256 devices in a mesh: ctx: 64 (over y, x_lo, z), tp: 4 (over x_hi, core).
Axes of the slice: x: 4 (x_hi: 2, x_lo: 2; x = x_hi * 2 + x_lo), y: 4, z: 8, core: 2. Of those that a mesh axis runs over, the one named last changes fastest.
Arguments:
- queries: bfloat16 [16384, 4096], P('ctx', 'tp'), may hold values from -8 to 8
- latent_keys: bfloat16 [512, 4096], P(('ctx', 'tp')), may hold values from -8 to 8
- latent_values: bfloat16 [512, 4096], P(('ctx', 'tp')), may hold values from -6 to 6
- gate_logit: float32 [], replicated, may hold values from 0.3 to 1.2
- last_frame: int32 [128], P('ctx'), may hold values from 0 to 7, as said below
- cotangent: bfloat16 [16384, 4096], P('ctx', 'tp'), may hold values from -6 to 6
Outputs:
- attended: bfloat16 [16384, 4096], P('ctx', 'tp')
- query_grad: bfloat16 [16384, 4096], P('ctx', 'tp')
- key_grad: float32 [512, 4096], P(('ctx', 'tp'))
- value_grad: float32 [512, 4096], P(('ctx', 'tp'))
The draws below stay inside these ranges and needn't reach their ends.
Inputs may be any that keep to these rules, and one draw needn't show every extreme that they name: Non-decreasing along the document; text block b sees the frames 0 to last_frame[b].
All inputs are finite; a program needn't handle non-finite values.
Results may differ from the reference program's by a relative error of at most 0.015.
Values may be sent and summed in bfloat16 or wider, within the bound.
No kernel may reach another device: no remote copies, remote signals or barrier semaphores. Data moves between devices by JAX's collectives and lax.ppermute only.
A program may use at most 64 MiB of HBM per device.

```python
import jax
import jax.numpy as jnp
from jax import lax

HEADS = 32
DH = 128
LATF = 64
TBLK = 128
FRAMES = 8
TOKENS = 16384
LATENTS = 512


def draw_latent_keys(key, part):
    key = jax.random.fold_in(key, 11)
    return jax.random.truncated_normal(key, -6.0, 6.0, (LATENTS, HEADS * DH), jnp.float32).astype(jnp.bfloat16)


def draw_queries(key, part):
    key = jax.random.fold_in(key, 12)
    return jax.random.truncated_normal(key, -6.0, 6.0, (TOKENS, HEADS * DH), jnp.float32).astype(jnp.bfloat16)


def draw_last_frame(key, part):
    key = jax.random.fold_in(key, 13)
    block_total = TOKENS // TBLK
    frame_marks = jax.random.permutation(key, block_total - 1)[:FRAMES - 1] + 1
    block_ids = jnp.arange(block_total, dtype=jnp.int32)
    return jnp.sum((frame_marks[None, :] <= block_ids[:, None]).astype(jnp.int32), axis=1).astype(jnp.int32)


def levels(key, shape, pieces, least, top_value):
    level = 1.0
    for axis_at, shards_of in pieces:
        draws = jax.random.uniform(jax.random.fold_in(jax.random.fold_in(key, 6), axis_at), (shards_of,), jnp.float32, least / len(pieces), top_value / len(pieces))
        level = level * jnp.repeat(jnp.exp(draws), shape[axis_at] // shards_of).reshape((-1,) + (1,) * (len(shape) - 1 - axis_at))
    return level


def scatter_about(stream_key, extent, scale, bound, pieces=(), held_as=jnp.bfloat16):
    array = jax.random.normal(stream_key, extent, jnp.float32) * scale
    if len(pieces) > 0:
        array = levels(stream_key, extent, pieces, -0.22, 0.18) * array
    return jnp.clip(array, min=-bound, max=bound).astype(held_as)


def setup_inputs(seed: int = 0) -> dict:
    splits = jax.random.split(jax.random.key(seed), 7)
    return {
        "queries": draw_queries(jax.random.fold_in(splits[6], 71), 0),
        "latent_keys": draw_latent_keys(jax.random.fold_in(splits[6], 71), 0),
        "latent_values": scatter_about(splits[2], (LATENTS, HEADS * DH), 1.0, 6.0, ((0, 256),)),
        "gate_logit": jnp.clip(jax.random.uniform(splits[3], (), jnp.float32, 0.3, 1.2), 0.3, 1.2),
        "last_frame": draw_last_frame(jax.random.fold_in(splits[6], 71), 0),
        "cotangent": scatter_about(splits[5], (TOKENS, HEADS * DH), 1.0, 6.0, ((0, 64), (1, 4))),
    }


masked_fill = -1.0e30


def reference(queries, latent_keys, latent_values, gate_logit, last_frame, cotangent):
    score_scale = 1.0 / (DH ** 0.5)
    gate_value = jnp.tanh(gate_logit.astype(jnp.float32))
    frame_index = (jnp.arange(LATENTS, dtype=jnp.int32) // LATF).astype(jnp.int32)
    last_tok = jnp.repeat(last_frame, TBLK, total_repeat_length=TOKENS)
    block_rows = min(1024, TOKENS)
    block_count = TOKENS // block_rows
    keys_heads = latent_keys.astype(jnp.float32).reshape(LATENTS, HEADS, DH)
    values_heads = latent_values.astype(jnp.float32).reshape(LATENTS, HEADS, DH)

    def advance(running, block_index):
        row_start = (block_index * block_rows).astype(jnp.int32)
        query_block = lax.dynamic_slice_in_dim(queries, row_start, block_rows, 0)
        query_block = query_block.astype(jnp.float32).reshape(block_rows, HEADS, DH)
        cot_block = lax.dynamic_slice_in_dim(cotangent, row_start, block_rows, 0).astype(jnp.float32)
        last_block = lax.dynamic_slice_in_dim(last_tok, row_start, block_rows, 0)
        visible = frame_index[None, :] <= last_block[:, None]
        scores = jnp.einsum("qhd,khd->hqk", query_block, keys_heads) * score_scale
        scores = jnp.where(visible[None], scores, masked_fill)
        maxima = jnp.max(scores, axis=-1, keepdims=True)
        expo = jnp.where(visible[None], jnp.exp(scores - maxima), 0.0)
        totals = jnp.sum(expo, axis=-1, keepdims=True)
        weights = expo / totals
        weights_low = weights.astype(jnp.bfloat16).astype(jnp.float32)
        context = jnp.einsum("hqk,khd->qhd", weights_low, values_heads).reshape(block_rows, HEADS * DH)
        attended = (gate_value * context).astype(jnp.bfloat16)
        gated_cot = (gate_value * cot_block).astype(jnp.bfloat16).astype(jnp.float32)
        gated_heads = gated_cot.reshape(block_rows, HEADS, DH)
        prob_grad = jnp.einsum("qhd,khd->hqk", gated_heads, values_heads)
        inner_sum = jnp.sum(weights * prob_grad, axis=-1, keepdims=True)
        score_grad = (weights * (prob_grad - inner_sum) * score_scale).astype(jnp.bfloat16).astype(jnp.float32)
        query_grad = jnp.einsum("hqk,khd->qhd", score_grad, keys_heads).reshape(block_rows, HEADS * DH)
        key_part = jnp.einsum("hqk,qhd->khd", score_grad, query_block)
        value_part = jnp.einsum("hqk,qhd->khd", weights_low, gated_heads)
        return (running[0] + key_part, running[1] + value_part), (attended, query_grad.astype(jnp.bfloat16))

    zeros_kv = jnp.zeros((LATENTS, HEADS, DH), jnp.float32)
    sums, outputs = lax.scan(advance, (zeros_kv, zeros_kv), jnp.arange(block_count, dtype=jnp.int32))
    attended = outputs[0].reshape(TOKENS, HEADS * DH)
    query_grad = outputs[1].reshape(TOKENS, HEADS * DH)
    key_grad = sums[0].reshape(LATENTS, HEADS * DH)
    value_grad = sums[1].reshape(LATENTS, HEADS * DH)
    return (attended, query_grad, key_grad, value_grad)
```

```python
import functools
import math

import jax
import jax.numpy as jnp
from jax import lax
from jax.experimental import pallas as pl
from jax.experimental.pallas import tpu as pltpu
from jax.sharding import PartitionSpec as P

DH = 128
LATF = 64
TBLK = 128
GROUP = 8
ZSIZE = 8
TP = 4
EXTRA = 16

masked_fill = -1e30
SCALE = 1.0 / DH**0.5
LOG2E = math.log2(math.e)
PARAMS = pltpu.CompilerParams(vmem_limit_bytes=32 * 2**20)
SMEM = pl.BlockSpec(memory_space=pltpu.SMEM)
VMEM = pl.BlockSpec(memory_space=pltpu.VMEM)


def pack_kernel(place_ref, last_ref, q_ref, c_ref, *out_refs):
    tok = q_ref.shape[0]
    group = place_ref[0]
    half = EXTRA // 2
    rows = lax.broadcasted_iota(jnp.int32, (EXTRA, DH), 0)
    frames = jnp.where(rows < half, last_ref[0], last_ref[1])
    frames = frames.astype(jnp.float32).astype(jnp.bfloat16)
    for k, out in enumerate(out_refs):
        cols = pl.ds(pl.multiple_of((group ^ k) * DH, DH), DH)
        out[0:tok, :] = q_ref[:, cols]
        out[tok : 2 * tok, :] = c_ref[:, cols]
        out[2 * tok : 2 * tok + EXTRA, :] = frames


def unpack_kernel(place_ref, *refs):
    block_refs, (att_ref, dq_ref) = refs[:GROUP], refs[GROUP:]
    tok = att_ref.shape[0]
    group = place_ref[0]
    for k, block in enumerate(block_refs):
        cols = pl.ds(pl.multiple_of((group ^ k) * DH, DH), DH)
        att_ref[:, cols] = block[0:tok, :]
        dq_ref[:, cols] = block[tok : 2 * tok, :]


def dot(a, b, dims):
    return lax.dot_general(a, b, (dims, ((), ())), preferred_element_type=jnp.float32)


def attention_kernel(gate_ref, k_ref, v_ref, *refs):
    msgs, outs = refs[:GROUP], refs[GROUP : 2 * GROUP]
    dk_ref, dv_ref, in_s, out_s, dk_s, dv_s = refs[2 * GROUP :]
    tok = outs[0].shape[0] // 2
    lat = k_ref.shape[0]
    gate = gate_ref[0]
    for j, msg in enumerate(msgs):
        in_s[j] = msg[...]
    dk_s[...] = jnp.zeros_like(dk_s)
    dv_s[...] = jnp.zeros_like(dv_s)
    frame = (lax.broadcasted_iota(jnp.int32, (1, lat), 1) // LATF).astype(jnp.float32)

    def step(j, carry):
        keys, values = k_ref[...], v_ref[...]
        q = in_s[j, 0:tok, :]
        cot = in_s[j, tok : 2 * tok, :]
        gcot = (gate * cot.astype(jnp.float32)).astype(jnp.bfloat16)
        scores = dot(q, keys, ((1,), (1,))) * (SCALE * LOG2E)
        parts = []
        for i in range(tok // TBLK):
            row = 2 * tok + i * (EXTRA // 2)
            last = in_s[j, row : row + 1, :].astype(jnp.float32)
            last = jnp.concatenate([last] * (lat // DH), axis=1)
            bias = jnp.where(frame <= last, 0.0, masked_fill)
            parts.append(scores[i * TBLK : (i + 1) * TBLK] + bias)
        scores = jnp.concatenate(parts, axis=0)
        expo = jnp.exp2(scores - jnp.max(scores, axis=-1, keepdims=True))
        weights = expo * (1.0 / jnp.sum(expo, axis=-1, keepdims=True))
        low = weights.astype(jnp.bfloat16)
        context = dot(low, values, ((1,), (0,)))
        out_s[j, 0:tok, :] = (gate * context).astype(jnp.bfloat16)
        prob_grad = dot(gcot, values, ((1,), (1,)))
        inner = jnp.sum(weights * prob_grad, axis=-1, keepdims=True)
        sgrad = (weights * (prob_grad - inner) * SCALE).astype(jnp.bfloat16)
        out_s[j, tok : 2 * tok, :] = dot(sgrad, keys, ((1,), (0,))).astype(jnp.bfloat16)
        dk_s[...] += dot(sgrad, q, ((0,), (0,)))
        dv_s[...] += dot(low, gcot, ((0,), (0,)))
        return carry

    lax.fori_loop(0, GROUP, step, 0)
    for j, out in enumerate(outs):
        out[...] = out_s[j]
    dk_ref[...] = dk_s[...].astype(jnp.bfloat16)
    dv_ref[...] = dv_s[...].astype(jnp.bfloat16)


def per_device(queries, latent_keys, latent_values, gate_logit, last_frame, cotangent):
    tok, columns = queries.shape
    own, wide = latent_keys.shape
    everyone = ("ctx", "tp")
    devices = GROUP * ZSIZE * TP
    lat = own * devices
    group = lax.axis_index("ctx") // ZSIZE
    place = group.astype(jnp.int32).reshape(1)
    gate = jnp.tanh(gate_logit).astype(jnp.float32).reshape(1)

    both = jnp.stack([latent_keys, latent_values]).reshape(2 * own, TP, GROUP, DH)
    both = both.transpose(2, 1, 0, 3)[:, None]
    both = jnp.broadcast_to(both, (GROUP, ZSIZE, TP, 2 * own, DH)).reshape(devices, 2 * own, DH)
    both = lax.all_to_all(both, everyone, 0, 0)
    keys = both[:, :own].reshape(lat, DH)
    values = both[:, own:].reshape(lat, DH)

    def swap(x, k):
        pairs = [(i, i ^ (k * ZSIZE)) for i in range(GROUP * ZSIZE)]
        return x if k == 0 else lax.ppermute(x, "ctx", pairs)

    msg_shape = jax.ShapeDtypeStruct((2 * tok + EXTRA, DH), jnp.bfloat16)
    back_shape = jax.ShapeDtypeStruct((2 * tok, DH), jnp.bfloat16)
    msgs = pl.pallas_call(
        pack_kernel,
        out_shape=[msg_shape] * GROUP,
        in_specs=[SMEM, SMEM, VMEM, VMEM],
        out_specs=[VMEM] * GROUP,
        compiler_params=PARAMS,
        name="pack",
    )(place, last_frame, queries, cotangent)
    msgs = [swap(m, k) for k, m in enumerate(msgs)]

    grad_shape = jax.ShapeDtypeStruct((lat, DH), jnp.bfloat16)
    *backs, key_terms, value_terms = pl.pallas_call(
        attention_kernel,
        out_shape=[back_shape] * GROUP + [grad_shape] * 2,
        in_specs=[SMEM] + [VMEM] * (2 + GROUP),
        out_specs=[VMEM] * (GROUP + 2),
        scratch_shapes=[
            pltpu.VMEM((GROUP, 2 * tok + EXTRA, DH), jnp.bfloat16),
            pltpu.VMEM((GROUP, 2 * tok, DH), jnp.bfloat16),
            pltpu.VMEM((lat, DH), jnp.float32),
            pltpu.VMEM((lat, DH), jnp.float32),
        ],
        compiler_params=PARAMS,
        name="attention",
    )(gate, keys, values, *msgs)

    terms = jnp.concatenate(
        [key_terms.reshape(devices, own, DH), value_terms.reshape(devices, own, DH)], axis=1
    )
    terms = lax.all_to_all(terms, everyone, 0, 0)
    backs = [swap(b, k) for k, b in enumerate(backs)]
    out_shape = jax.ShapeDtypeStruct((tok, columns), jnp.bfloat16)
    attended, query_grad = pl.pallas_call(
        unpack_kernel,
        out_shape=[out_shape] * 2,
        in_specs=[SMEM] + [VMEM] * GROUP,
        out_specs=[VMEM] * 2,
        compiler_params=PARAMS,
        name="unpack",
    )(place, *backs)
    sums = jnp.sum(
        terms.astype(jnp.float32).reshape(GROUP, ZSIZE, TP, 2 * own, DH), axis=1
    )
    sums = sums.transpose(2, 1, 0, 3).reshape(2, own, wide)
    return (attended, query_grad, sums[0], sums[1])


def solution(mesh):
    placed = (
        P("ctx", "tp"),
        P(("ctx", "tp"), None),
        P(("ctx", "tp"), None),
        P(),
        P("ctx"),
        P("ctx", "tp"),
    )
    return jax.shard_map(
        per_device,
        mesh=mesh,
        in_specs=placed,
        out_specs=(P("ctx", "tp"), P("ctx", "tp"), P(("ctx", "tp"), None), P(("ctx", "tp"), None)),
        check_vma=False,
    )
```

```python
import functools
import math

import jax
import jax.numpy as jnp
from jax import lax
from jax.experimental import pallas as pl
from jax.experimental.pallas import tpu as pltpu
from jax.sharding import Mesh, PartitionSpec as P

DH = 128
TBLK = 128
BLOCKS = 2
GROUP = 4
HALVES = 2
ZSIZE = 8
TP = 4
SIZES = {"h": HALVES, "g": GROUP, "z": ZSIZE, "tp": TP}
AXES = tuple(SIZES)
ORDER = ("h", "g", "z", "tp")
UNPACK = 0
EXTRA = 16

masked_fill = -1e30
SCALE = 1.0 / DH**0.5
LOG2E = math.log2(math.e)
PARAMS = pltpu.CompilerParams(vmem_limit_bytes=32 * 2**20)
SMEM = pl.BlockSpec(memory_space=pltpu.SMEM)
VMEM = pl.BlockSpec(memory_space=pltpu.VMEM)


def stride(axis):
    return math.prod(SIZES[a] for a in ORDER[ORDER.index(axis) + 1 :])


def source(**at):
    return sum(i * stride(axis) for axis, i in at.items())


def pack_kernel(place_ref, last_ref, q_ref, c_ref, *out_refs):
    tok, width = q_ref.shape[0], out_refs[0].shape[1]
    half = EXTRA // 2
    rows = lax.broadcasted_iota(jnp.int32, (EXTRA, width), 0)
    frames = jnp.where(rows < half, last_ref[0], last_ref[1])
    frames = frames.astype(jnp.float32).astype(jnp.bfloat16)
    for k, out in enumerate(out_refs):
        cols = pl.ds(pl.multiple_of((place_ref[0] ^ k) * width, width), width)
        out[0:tok, :] = q_ref[:, cols]
        out[tok : 2 * tok, :] = c_ref[:, cols]
        out[2 * tok : 2 * tok + EXTRA, :] = frames


def unpack_kernel(place_ref, *refs):
    block_refs, (att_ref, dq_ref) = refs[:GROUP], refs[GROUP:]
    tok, width = att_ref.shape[0], block_refs[0].shape[1]
    for k, block in enumerate(block_refs):
        cols = pl.ds(pl.multiple_of((place_ref[0] ^ k) * width, width), width)
        att_ref[:, cols] = block[0:tok, :]
        dq_ref[:, cols] = block[tok : 2 * tok, :]


def settle_kernel(in_ref, k_ref, v_ref):
    own, wide = k_ref.shape
    width = in_ref.shape[2]
    for g in range(GROUP):
        for t in range(TP):
            total = jnp.zeros((2 * own, width), jnp.float32)
            for h in range(HALVES):
                for z in range(ZSIZE):
                    total += in_ref[source(h=h, g=g, z=z, tp=t)].astype(jnp.float32)
            col = (t * GROUP + g) * width
            k_ref[:, col : col + width] = total[0:own]
            v_ref[:, col : col + width] = total[own:]


def dot(a, b, dims):
    return lax.dot_general(a, b, (dims, ((), ())), preferred_element_type=jnp.float32)


def attention_kernel(gate_ref, kv_ref, *refs):
    msgs, outs = refs[:GROUP], refs[GROUP : 2 * GROUP]
    grad_ref, k_s, v_s, dk_s, dv_s = refs[2 * GROUP :]
    tok = outs[0].shape[0] // 2
    lat, width = k_s.shape
    own = kv_ref.shape[1] // 2
    gate = gate_ref[0]
    k_s[...] = kv_ref[:, 0:own, :].reshape(lat, width)
    v_s[...] = kv_ref[:, own : 2 * own, :].reshape(lat, width)
    place = lax.broadcasted_iota(jnp.int32, (1, lat), 1) // own
    frame = place // stride("h") % HALVES * GROUP + place // stride("g") % GROUP
    frame = frame.astype(jnp.float32)

    def bias(msg, i):
        row = 2 * tok + i * (EXTRA // 2)
        last = msg[row : row + 1, 0:DH].astype(jnp.float32)
        return jnp.where(frame <= jnp.concatenate([last] * (lat // DH), axis=1), 0.0, masked_fill)

    def step(first):
        blocks = range(first, first + BLOCKS)
        biases = [bias(msgs[j], i) for j in blocks for i in range(tok // TBLK)]
        heads = []
        for h in range(width // DH):
            cols = slice(h * DH, (h + 1) * DH)
            q = jnp.concatenate([msgs[j][0:tok, cols] for j in blocks], axis=0)
            cot = jnp.concatenate([msgs[j][tok : 2 * tok, cols] for j in blocks], axis=0)
            gcot = (gate * cot.astype(jnp.float32)).astype(jnp.bfloat16)
            heads.append((cols, q, gcot, k_s[:, cols], v_s[:, cols]))

        def softmax(head):
            _, q, _, keys, _ = head
            scores = dot(q, keys, ((1,), (1,)))
            parts = [
                scores[i * TBLK : (i + 1) * TBLK] * (SCALE * LOG2E) + b for i, b in enumerate(biases)
            ]
            scores = jnp.concatenate(parts, axis=0)
            expo = jnp.exp2(scores - jnp.max(scores, axis=-1, keepdims=True))
            return expo * (1.0 / jnp.sum(expo, axis=-1, keepdims=True))

        def prob_grads(head):
            _, _, gcot, _, values = head
            return dot(gcot, values, ((1,), (1,)))

        def score_grads(weights, grads):
            inner = jnp.sum(weights * grads, axis=-1, keepdims=True)
            return (weights * (grads - inner)).astype(jnp.bfloat16)

        def finish(head, low, sgrad):
            cols, q, gcot, keys, values = head
            out = (gate * dot(low, values, ((1,), (0,)))).astype(jnp.bfloat16)
            for i, j in enumerate(blocks):
                outs[j][0:tok, cols] = out[i * tok : (i + 1) * tok]
            out = (SCALE * dot(sgrad, keys, ((1,), (0,)))).astype(jnp.bfloat16)
            for i, j in enumerate(blocks):
                outs[j][tok : 2 * tok, cols] = out[i * tok : (i + 1) * tok]
            dk = dot(sgrad, q, ((0,), (0,)))
            dv = dot(low, gcot, ((0,), (0,)))
            dk_s[:, cols] = dk if first == 0 else dk_s[:, cols] + dk
            dv_s[:, cols] = dv if first == 0 else dv_s[:, cols] + dv

        one, two = heads
        weights1, grads1 = softmax(one), prob_grads(one)
        weights2 = softmax(two)
        low1, sgrad1 = weights1.astype(jnp.bfloat16), score_grads(weights1, grads1)
        grads2 = prob_grads(two)
        finish(one, low1, sgrad1)
        low2, sgrad2 = weights2.astype(jnp.bfloat16), score_grads(weights2, grads2)
        finish(two, low2, sgrad2)

    for first in range(0, GROUP, BLOCKS):
        step(first)
    for i, grads in enumerate((SCALE * dk_s[...], dv_s[...])):
        piece = grads.astype(jnp.bfloat16).reshape(lat // own, own, width)
        grad_ref[:, i * own : (i + 1) * own, :] = piece


def cut_kernel(k_ref, v_ref, out_ref):
    width = out_ref.shape[2]
    for t in range(TP):
        for g in range(GROUP):
            col = (t * GROUP + g) * width
            piece = jnp.concatenate([k_ref[:, col : col + width], v_ref[:, col : col + width]], axis=0)
            for h in range(HALVES):
                for z in range(ZSIZE):
                    out_ref[source(h=h, g=g, z=z, tp=t)] = piece


def call(kernel, shapes, specs, *args, cost=0, **kwargs):
    if cost:
        kwargs["cost_estimate"] = pl.CostEstimate(flops=cost, bytes_accessed=0, transcendentals=0)
    name = kernel.__name__.removesuffix("_kernel")
    out_specs = [VMEM] * len(shapes)
    return pl.pallas_call(
        kernel,
        out_shape=shapes,
        in_specs=specs,
        out_specs=out_specs,
        compiler_params=PARAMS,
        name=name,
        **kwargs,
    )(*args)


def swap(x, axis, size, k):
    return x if k == 0 else lax.ppermute(x, axis, [(i, i ^ k) for i in range(size)])


def per_device(queries, latent_keys, latent_values, gate_logit, last_frame, cotangent):
    tok, columns = queries.shape
    own, wide = latent_keys.shape
    width = columns // GROUP
    devices = HALVES * GROUP * ZSIZE * TP
    lat = own * devices
    place = lax.axis_index("g").astype(jnp.int32).reshape(1)
    gate = jnp.tanh(gate_logit).astype(jnp.float32).reshape(1)

    def low(*shape):
        return jax.ShapeDtypeStruct(shape, jnp.bfloat16)

    (both,) = call(
        cut_kernel, [low(devices, 2 * own, width)], [VMEM] * 2, latent_keys, latent_values
    )
    both = lax.all_to_all(both, ORDER, 0, 0)

    msgs = call(
        pack_kernel,
        [low(2 * tok + EXTRA, width)] * GROUP,
        [SMEM, SMEM, VMEM, VMEM],
        place,
        last_frame,
        queries,
        cotangent,
    )
    msgs = [swap(x, "g", GROUP, k) for k, x in enumerate(msgs)]

    *backs, terms = call(
        attention_kernel,
        [low(2 * tok, width)] * GROUP + [low(devices, 2 * own, width)],
        [SMEM] + [VMEM] * (1 + GROUP),
        gate,
        both,
        *msgs,
        scratch_shapes=[
            pltpu.VMEM((lat, width), jnp.bfloat16),
            pltpu.VMEM((lat, width), jnp.bfloat16),
            pltpu.VMEM((lat, width), jnp.float32),
            pltpu.VMEM((lat, width), jnp.float32),
        ],
    )

    terms = lax.all_to_all(terms, ORDER, 0, 0)
    grad = jax.ShapeDtypeStruct((own, wide), jnp.float32)
    key_grad, value_grad = call(settle_kernel, [grad] * 2, [VMEM], terms)

    backs = [swap(x, "g", GROUP, k) for k, x in enumerate(backs)]
    attended, query_grad = call(
        unpack_kernel, [low(tok, columns)] * 2, [SMEM] + [VMEM] * GROUP, place, *backs, cost=UNPACK
    )
    return (attended, query_grad, key_grad, value_grad)


def solution(mesh):
    fine = Mesh(mesh.devices.reshape(tuple(SIZES.values())), AXES)
    tokens = P(AXES[:3], "tp")
    rows = P(AXES, None)
    return jax.shard_map(
        per_device,
        mesh=fine,
        in_specs=(tokens, rows, rows, P(), P(AXES[:3]), tokens),
        out_specs=(tokens, tokens, rows, rows),
        check_vma=False,
    )
```

```python
import functools
import math

import jax
import jax.numpy as jnp
from jax import lax
from jax.experimental import pallas as pl
from jax.experimental.pallas import tpu as pltpu
from jax.sharding import Mesh, PartitionSpec as P

DH = 128
TBLK = 128
BLOCKS = 2
GROUP = 4
HALVES = 2
ZSIZE = 8
TP = 4
SIZES = {"h": HALVES, "g": GROUP, "z": ZSIZE, "tp": TP}
AXES = tuple(SIZES)
ORDER = ("h", "g", "z", "tp")
MERGE = 10**11
EARLY = (3,)
UNPACK = 0
EXTRA = 16

masked_fill = -1e30
SCALE = 1.0 / DH**0.5
LOG2E = math.log2(math.e)
PARAMS = pltpu.CompilerParams(vmem_limit_bytes=32 * 2**20)
SMEM = pl.BlockSpec(memory_space=pltpu.SMEM)
VMEM = pl.BlockSpec(memory_space=pltpu.VMEM)
HBM = pl.BlockSpec(memory_space=pltpu.HBM)


def stride(axis):
    return math.prod(SIZES[a] for a in ORDER[ORDER.index(axis) + 1 :])


def source(**at):
    return sum(i * stride(axis) for axis, i in at.items())


def columns_of(k, width):
    return pl.ds(pl.multiple_of((lax.axis_index("g") ^ k) * width, width), width)


def prepare_kernel(last_ref, k_ref, v_ref, q_ref, c_ref, kv_out, *refs):
    outs, (last_s, k_s, v_s, last_sem, kv_sems, sems) = refs[:GROUP], refs[GROUP:]
    tok, width = q_ref.shape[0], outs[0].shape[1]
    small = [
        pltpu.make_async_copy(k_ref, k_s, kv_sems.at[0]),
        pltpu.make_async_copy(v_ref, v_s, kv_sems.at[1]),
        pltpu.make_async_copy(last_ref, last_s, last_sem),
    ]
    large = []
    for k, out in enumerate(outs):
        cols = columns_of(k, width)
        for i, ref in enumerate((q_ref, c_ref)):
            rows = pl.ds(i * tok, tok)
            large.append(pltpu.make_async_copy(ref.at[:, cols], out.at[rows, :], sems.at[2 * k + i]))
    for copy in small + large:
        copy.start()
    small[0].wait()
    small[1].wait()
    for t in range(TP):
        for g in range(GROUP):
            col = (t * GROUP + g) * width
            piece = jnp.concatenate([k_s[:, col : col + width], v_s[:, col : col + width]], axis=0)
            for h in range(HALVES):
                for z in range(ZSIZE):
                    kv_out[source(h=h, g=g, z=z, tp=t)] = piece
    small[2].wait()
    rows = lax.broadcasted_iota(jnp.int32, (EXTRA, width), 0)
    frames = jnp.where(rows < EXTRA // 2, last_s[0], last_s[1])
    frames = frames.astype(jnp.float32).astype(jnp.bfloat16)
    for out in outs:
        out[2 * tok : 2 * tok + EXTRA, :] = frames
    for copy in large:
        copy.wait()


def merge_kernel(*refs):
    for j, ref in enumerate(refs[:-1]):
        refs[-1][j] = ref[...]


def unpack_kernel(*refs):
    blocks, (att_ref, dq_ref, sems) = refs[:GROUP], refs[GROUP:]
    tok, width = att_ref.shape[0], blocks[0].shape[1]
    copies = []
    for k, block in enumerate(blocks):
        for i, out in enumerate((att_ref, dq_ref)):
            rows = pl.ds(i * tok, tok)
            cols = columns_of(k, width)
            copies.append(pltpu.make_async_copy(block.at[rows, :], out.at[:, cols], sems.at[2 * k + i]))
    for copy in copies:
        copy.start()
    for copy in copies:
        copy.wait()


def settle_kernel(in_ref, k_ref, v_ref):
    own, wide = k_ref.shape
    width = in_ref.shape[2]
    for g in range(GROUP):
        for t in range(TP):
            total = jnp.zeros((2 * own, width), jnp.float32)
            for h in range(HALVES):
                for z in range(ZSIZE):
                    total += in_ref[source(h=h, g=g, z=z, tp=t)].astype(jnp.float32)
            col = (t * GROUP + g) * width
            k_ref[:, col : col + width] = total[0:own]
            v_ref[:, col : col + width] = total[own:]


def dot(a, b, dims):
    return lax.dot_general(a, b, (dims, ((), ())), preferred_element_type=jnp.float32)


def attention_kernel(gate_ref, kv_ref, early_ref, *refs):
    late = GROUP - len(EARLY)
    late_refs, outs = refs[:late], refs[late : late + GROUP]
    grad_ref, k_s, v_s, dk_s, dv_s = refs[late + GROUP :]
    msgs = {k: early_ref.at[i] for i, k in enumerate(EARLY)}
    msgs |= zip((k for k in range(GROUP) if k not in EARLY), late_refs)
    tok = outs[0].shape[0] // 2
    lat, width = k_s.shape
    own = kv_ref.shape[1] // 2
    gate = gate_ref[0]
    k_s[...] = kv_ref[:, 0:own, :].reshape(lat, width)
    v_s[...] = kv_ref[:, own : 2 * own, :].reshape(lat, width)
    place = lax.broadcasted_iota(jnp.int32, (1, lat), 1) // own
    frame = place // stride("h") % HALVES * GROUP + place // stride("g") % GROUP
    frame = frame.astype(jnp.float32)

    def bias(j, i):
        row = 2 * tok + i * (EXTRA // 2)
        last = msgs[j][row : row + 1, 0:DH].astype(jnp.float32)
        return jnp.where(frame <= jnp.concatenate([last] * (lat // DH), axis=1), 0.0, masked_fill)

    def step(first):
        blocks = range(first, first + BLOCKS)
        biases = [bias(j, i) for j in blocks for i in range(tok // TBLK)]
        heads = []
        for h in range(width // DH):
            cols = slice(h * DH, (h + 1) * DH)
            q = jnp.concatenate([msgs[j][0:tok, cols] for j in blocks], axis=0)
            cot = jnp.concatenate([msgs[j][tok : 2 * tok, cols] for j in blocks], axis=0)
            gcot = (gate * cot.astype(jnp.float32)).astype(jnp.bfloat16)
            heads.append((cols, q, gcot, k_s[:, cols], v_s[:, cols]))

        def softmax(head):
            _, q, _, keys, _ = head
            scores = dot(q, keys, ((1,), (1,)))
            parts = [
                scores[i * TBLK : (i + 1) * TBLK] * (SCALE * LOG2E) + b for i, b in enumerate(biases)
            ]
            scores = jnp.concatenate(parts, axis=0)
            expo = jnp.exp2(scores - jnp.max(scores, axis=-1, keepdims=True))
            return expo * (1.0 / jnp.sum(expo, axis=-1, keepdims=True))

        def prob_grads(head):
            _, _, gcot, _, values = head
            return dot(gcot, values, ((1,), (1,)))

        def score_grads(weights, grads):
            inner = jnp.sum(weights * grads, axis=-1, keepdims=True)
            return (weights * (grads - inner)).astype(jnp.bfloat16)

        def finish(head, low, sgrad):
            cols, q, gcot, keys, values = head
            out = (gate * dot(low, values, ((1,), (0,)))).astype(jnp.bfloat16)
            for i, j in enumerate(blocks):
                outs[j][0:tok, cols] = out[i * tok : (i + 1) * tok]
            out = (SCALE * dot(sgrad, keys, ((1,), (0,)))).astype(jnp.bfloat16)
            for i, j in enumerate(blocks):
                outs[j][tok : 2 * tok, cols] = out[i * tok : (i + 1) * tok]
            dk = dot(sgrad, q, ((0,), (0,)))
            dv = dot(low, gcot, ((0,), (0,)))
            dk_s[:, cols] = dk if first == 0 else dk_s[:, cols] + dk
            dv_s[:, cols] = dv if first == 0 else dv_s[:, cols] + dv

        one, two = heads
        weights1, grads1 = softmax(one), prob_grads(one)
        weights2 = softmax(two)
        low1, sgrad1 = weights1.astype(jnp.bfloat16), score_grads(weights1, grads1)
        grads2 = prob_grads(two)
        finish(one, low1, sgrad1)
        low2, sgrad2 = weights2.astype(jnp.bfloat16), score_grads(weights2, grads2)
        finish(two, low2, sgrad2)

    for first in range(0, GROUP, BLOCKS):
        step(first)
    for i, grads in enumerate((SCALE * dk_s[...], dv_s[...])):
        piece = grads.astype(jnp.bfloat16).reshape(lat // own, own, width)
        grad_ref[:, i * own : (i + 1) * own, :] = piece


def call(kernel, shapes, specs, *args, cost=0, out_spec=VMEM, **kwargs):
    if cost:
        kwargs["cost_estimate"] = pl.CostEstimate(flops=cost, bytes_accessed=0, transcendentals=0)
    name = kernel.__name__.removesuffix("_kernel")
    out_specs = [out_spec] * len(shapes)
    return pl.pallas_call(
        kernel,
        out_shape=shapes,
        in_specs=specs,
        out_specs=out_specs,
        compiler_params=PARAMS,
        name=name,
        **kwargs,
    )(*args)


def swap(x, axis, size, k):
    return x if k == 0 else lax.ppermute(x, axis, [(i, i ^ k) for i in range(size)])


def per_device(queries, latent_keys, latent_values, gate_logit, last_frame, cotangent):
    tok, columns = queries.shape
    own, wide = latent_keys.shape
    width = columns // GROUP
    devices = HALVES * GROUP * ZSIZE * TP
    lat = own * devices
    gate = jnp.tanh(gate_logit).astype(jnp.float32).reshape(1)

    def low(*shape):
        return jax.ShapeDtypeStruct(shape, jnp.bfloat16)

    kv_shape = low(devices, 2 * own, width)
    last_frame, latent_keys, latent_values, queries, cotangent = (
        pltpu.with_memory_space_constraint(x, pltpu.HBM)
        for x in (last_frame, latent_keys, latent_values, queries, cotangent)
    )
    both, *msgs = call(
        prepare_kernel,
        [kv_shape] + [low(2 * tok + EXTRA, width)] * GROUP,
        [HBM] * 5,
        last_frame,
        latent_keys,
        latent_values,
        queries,
        cotangent,
        scratch_shapes=[
            pltpu.SMEM((last_frame.shape[0],), jnp.int32),
            pltpu.VMEM((own, wide), jnp.bfloat16),
            pltpu.VMEM((own, wide), jnp.bfloat16),
            pltpu.SemaphoreType.DMA,
            pltpu.SemaphoreType.DMA((2,)),
            pltpu.SemaphoreType.DMA((2 * GROUP,)),
        ],
    )
    both = lax.all_to_all(both, ORDER, 0, 0)
    msgs = [swap(x, "g", GROUP, k) for k, x in enumerate(msgs)]
    early = low(len(EARLY), 2 * tok + EXTRA, width)
    early_msgs = [msgs[k] for k in EARLY]
    (early,) = call(merge_kernel, [early], [VMEM] * len(EARLY), *early_msgs, cost=MERGE)
    late_msgs = [x for k, x in enumerate(msgs) if k not in EARLY]

    *backs, terms = call(
        attention_kernel,
        [low(2 * tok, width)] * GROUP + [kv_shape],
        [SMEM] + [VMEM] * (2 + len(late_msgs)),
        gate,
        both,
        early,
        *late_msgs,
        scratch_shapes=[
            pltpu.VMEM((lat, width), jnp.bfloat16),
            pltpu.VMEM((lat, width), jnp.bfloat16),
            pltpu.VMEM((lat, width), jnp.float32),
            pltpu.VMEM((lat, width), jnp.float32),
        ],
    )

    terms = lax.all_to_all(terms, ORDER, 0, 0)
    grad = jax.ShapeDtypeStruct((own, wide), jnp.float32)
    key_grad, value_grad = call(settle_kernel, [grad] * 2, [VMEM], terms)

    backs = [swap(x, "g", GROUP, k) for k, x in enumerate(backs)]
    attended, query_grad = call(
        unpack_kernel,
        [low(tok, columns)] * 2,
        [VMEM] * GROUP,
        *backs,
        cost=UNPACK,
        out_spec=HBM,
        scratch_shapes=[pltpu.SemaphoreType.DMA((2 * GROUP,))],
    )
    return (attended, query_grad, key_grad, value_grad)


def solution(mesh):
    fine = Mesh(mesh.devices.reshape(tuple(SIZES.values())), AXES)
    tokens = P(AXES[:3], "tp")
    rows = P(AXES, None)
    return jax.shard_map(
        per_device,
        mesh=fine,
        in_specs=(tokens, rows, rows, P(), P(AXES[:3]), tokens),
        out_specs=(tokens, tokens, rows, rows),
        check_vma=False,
    )
```

```python
import functools
import math

import jax
import jax.numpy as jnp
from jax import lax
from jax.experimental import pallas as pl
from jax.experimental.pallas import tpu as pltpu
from jax.sharding import Mesh, PartitionSpec as P

DH = 128
TBLK = 128
BLOCKS = 2
GROUP = 4
HALVES = 2
ZSIZE = 8
TP = 4
SIZES = {"h": HALVES, "g": GROUP, "z": ZSIZE, "tp": TP}
AXES = tuple(SIZES)
ORDER = ("h", "g", "z", "tp")
MERGE = 10**11
EARLY = (3,)
UNPACK = 0
EXTRA = 16

masked_fill = -1e30
SCALE = 1.0 / DH**0.5
LOG2E = math.log2(math.e)
PARAMS = pltpu.CompilerParams(vmem_limit_bytes=32 * 2**20)
SMEM = pl.BlockSpec(memory_space=pltpu.SMEM)
VMEM = pl.BlockSpec(memory_space=pltpu.VMEM)
HBM = pl.BlockSpec(memory_space=pltpu.HBM)


def stride(axis):
    return math.prod(SIZES[a] for a in ORDER[ORDER.index(axis) + 1 :])


def source(**at):
    return sum(i * stride(axis) for axis, i in at.items())


def columns_of(k, width):
    return pl.ds(pl.multiple_of((lax.axis_index("g") ^ k) * width, width), width)


def prepare_kernel(last_ref, k_ref, v_ref, q_ref, c_ref, kv_out, *refs):
    outs, (last_s, k_s, v_s, last_sem, kv_sems, sems) = refs[:GROUP], refs[GROUP:]
    tok, width = q_ref.shape[0], outs[0].shape[1]
    small = [
        pltpu.make_async_copy(k_ref, k_s, kv_sems.at[0]),
        pltpu.make_async_copy(v_ref, v_s, kv_sems.at[1]),
        pltpu.make_async_copy(last_ref, last_s, last_sem),
    ]
    large = []
    for k, out in enumerate(outs):
        cols = columns_of(k, width)
        for i, ref in enumerate((q_ref, c_ref)):
            rows = pl.ds(i * tok, tok)
            large.append(pltpu.make_async_copy(ref.at[:, cols], out.at[rows, :], sems.at[2 * k + i]))
    for copy in small + large:
        copy.start()
    small[0].wait()
    small[1].wait()
    for t in range(TP):
        for g in range(GROUP):
            col = (t * GROUP + g) * width
            piece = jnp.concatenate([k_s[:, col : col + width], v_s[:, col : col + width]], axis=1)
            for h in range(HALVES):
                for z in range(ZSIZE):
                    kv_out[source(h=h, g=g, z=z, tp=t)] = piece
    small[2].wait()
    rows = lax.broadcasted_iota(jnp.int32, (EXTRA, width), 0)
    frames = jnp.where(rows < EXTRA // 2, last_s[0], last_s[1])
    frames = frames.astype(jnp.float32).astype(jnp.bfloat16)
    for out in outs:
        out[2 * tok : 2 * tok + EXTRA, :] = frames
    for copy in large:
        copy.wait()


def merge_kernel(*refs):
    for j, ref in enumerate(refs[:-1]):
        refs[-1][j] = ref[...]


def unpack_kernel(*refs):
    blocks, (att_ref, dq_ref, sems) = refs[:GROUP], refs[GROUP:]
    tok, width = att_ref.shape[0], blocks[0].shape[1]
    copies = []
    for k, block in enumerate(blocks):
        for i, out in enumerate((att_ref, dq_ref)):
            rows = pl.ds(i * tok, tok)
            cols = columns_of(k, width)
            copies.append(pltpu.make_async_copy(block.at[rows, :], out.at[:, cols], sems.at[2 * k + i]))
    for copy in copies:
        copy.start()
    for copy in copies:
        copy.wait()


def settle_kernel(in_ref, k_ref, v_ref):
    width = in_ref.shape[2] // 2
    for g in range(GROUP):
        for t in range(TP):
            total = jnp.zeros(in_ref.shape[1:], jnp.float32)
            for h in range(HALVES):
                for z in range(ZSIZE):
                    total += in_ref[source(h=h, g=g, z=z, tp=t)].astype(jnp.float32)
            col = (t * GROUP + g) * width
            k_ref[:, col : col + width] = total[:, 0:width]
            v_ref[:, col : col + width] = total[:, width:]


def dot(a, b, dims):
    return lax.dot_general(a, b, (dims, ((), ())), preferred_element_type=jnp.float32)


def attention_kernel(gate_ref, kv_ref, early_ref, *refs):
    late = GROUP - len(EARLY)
    late_refs, outs = refs[:late], refs[late : late + GROUP]
    grad_ref, k_s, v_s, dk_s, dv_s = refs[late + GROUP :]
    msgs = {k: early_ref.at[i] for i, k in enumerate(EARLY)}
    msgs |= zip((k for k in range(GROUP) if k not in EARLY), late_refs)
    tok = outs[0].shape[0] // 2
    lat, width = k_s.shape
    own = kv_ref.shape[1]
    gate = gate_ref[0]
    k_s[...] = kv_ref[:, :, 0:width].reshape(lat, width)
    v_s[...] = kv_ref[:, :, width:].reshape(lat, width)
    place = lax.broadcasted_iota(jnp.int32, (1, lat), 1) // own
    frame = place // stride("h") % HALVES * GROUP + place // stride("g") % GROUP
    frame = frame.astype(jnp.float32)

    def bias(j, i):
        row = 2 * tok + i * (EXTRA // 2)
        last = msgs[j][row : row + 1, 0:DH].astype(jnp.float32)
        return jnp.where(frame <= jnp.concatenate([last] * (lat // DH), axis=1), 0.0, masked_fill)

    def step(first):
        blocks = range(first, first + BLOCKS)
        biases = [bias(j, i) for j in blocks for i in range(tok // TBLK)]
        heads = []
        for h in range(width // DH):
            cols = slice(h * DH, (h + 1) * DH)
            q = jnp.concatenate([msgs[j][0:tok, cols] for j in blocks], axis=0)
            cot = jnp.concatenate([msgs[j][tok : 2 * tok, cols] for j in blocks], axis=0)
            gcot = (gate * cot.astype(jnp.float32)).astype(jnp.bfloat16)
            heads.append((cols, q, gcot, k_s[:, cols], v_s[:, cols]))

        def softmax(head):
            _, q, _, keys, _ = head
            scores = dot(q, keys, ((1,), (1,)))
            parts = [
                scores[i * TBLK : (i + 1) * TBLK] * (SCALE * LOG2E) + b for i, b in enumerate(biases)
            ]
            scores = jnp.concatenate(parts, axis=0)
            expo = jnp.exp2(scores - jnp.max(scores, axis=-1, keepdims=True))
            return expo * (1.0 / jnp.sum(expo, axis=-1, keepdims=True))

        def prob_grads(head):
            _, _, gcot, _, values = head
            return dot(gcot, values, ((1,), (1,)))

        def score_grads(weights, grads):
            inner = jnp.sum(weights * grads, axis=-1, keepdims=True)
            return (weights * (grads - inner)).astype(jnp.bfloat16)

        def finish(head, low, sgrad):
            cols, q, gcot, keys, values = head
            out = (gate * dot(low, values, ((1,), (0,)))).astype(jnp.bfloat16)
            for i, j in enumerate(blocks):
                outs[j][0:tok, cols] = out[i * tok : (i + 1) * tok]
            out = (SCALE * dot(sgrad, keys, ((1,), (0,)))).astype(jnp.bfloat16)
            for i, j in enumerate(blocks):
                outs[j][tok : 2 * tok, cols] = out[i * tok : (i + 1) * tok]
            dk = dot(q.T, sgrad, ((1,), (0,)))
            dv = dot(gcot.T, low, ((1,), (0,)))
            dk_s[cols, :] = dk if first == 0 else dk_s[cols, :] + dk
            dv_s[cols, :] = dv if first == 0 else dv_s[cols, :] + dv

        one, two = heads
        weights1, grads1 = softmax(one), prob_grads(one)
        weights2 = softmax(two)
        low1, sgrad1 = weights1.astype(jnp.bfloat16), score_grads(weights1, grads1)
        grads2 = prob_grads(two)
        finish(one, low1, sgrad1)
        low2, sgrad2 = weights2.astype(jnp.bfloat16), score_grads(weights2, grads2)
        finish(two, low2, sgrad2)

    for first in range(0, GROUP, BLOCKS):
        step(first)
    for i, grads in enumerate((SCALE * dk_s[...], dv_s[...])):
        piece = grads.T.astype(jnp.bfloat16).reshape(lat // own, own, width)
        grad_ref[:, :, i * width : (i + 1) * width] = piece


def call(kernel, shapes, specs, *args, cost=0, out_spec=VMEM, **kwargs):
    if cost:
        kwargs["cost_estimate"] = pl.CostEstimate(flops=cost, bytes_accessed=0, transcendentals=0)
    name = kernel.__name__.removesuffix("_kernel")
    out_specs = [out_spec] * len(shapes)
    return pl.pallas_call(
        kernel,
        out_shape=shapes,
        in_specs=specs,
        out_specs=out_specs,
        compiler_params=PARAMS,
        name=name,
        **kwargs,
    )(*args)


def swap(x, axis, size, k):
    return x if k == 0 else lax.ppermute(x, axis, [(i, i ^ k) for i in range(size)])


def per_device(queries, latent_keys, latent_values, gate_logit, last_frame, cotangent):
    tok, columns = queries.shape
    own, wide = latent_keys.shape
    width = columns // GROUP
    devices = HALVES * GROUP * ZSIZE * TP
    lat = own * devices
    gate = jnp.tanh(gate_logit).astype(jnp.float32).reshape(1)

    def low(*shape):
        return jax.ShapeDtypeStruct(shape, jnp.bfloat16)

    kv_shape = low(devices, own, 2 * width)
    last_frame, latent_keys, latent_values, queries, cotangent = (
        pltpu.with_memory_space_constraint(x, pltpu.HBM)
        for x in (last_frame, latent_keys, latent_values, queries, cotangent)
    )
    both, *msgs = call(
        prepare_kernel,
        [kv_shape] + [low(2 * tok + EXTRA, width)] * GROUP,
        [HBM] * 5,
        last_frame,
        latent_keys,
        latent_values,
        queries,
        cotangent,
        scratch_shapes=[
            pltpu.SMEM((last_frame.shape[0],), jnp.int32),
            pltpu.VMEM((own, wide), jnp.bfloat16),
            pltpu.VMEM((own, wide), jnp.bfloat16),
            pltpu.SemaphoreType.DMA,
            pltpu.SemaphoreType.DMA((2,)),
            pltpu.SemaphoreType.DMA((2 * GROUP,)),
        ],
    )
    both = lax.all_to_all(both, ORDER, 0, 0)
    msgs = [swap(x, "g", GROUP, k) for k, x in enumerate(msgs)]
    early = low(len(EARLY), 2 * tok + EXTRA, width)
    early_msgs = [msgs[k] for k in EARLY]
    (early,) = call(merge_kernel, [early], [VMEM] * len(EARLY), *early_msgs, cost=MERGE)
    late_msgs = [x for k, x in enumerate(msgs) if k not in EARLY]

    *backs, terms = call(
        attention_kernel,
        [low(2 * tok, width)] * GROUP + [kv_shape],
        [SMEM] + [VMEM] * (2 + len(late_msgs)),
        gate,
        both,
        early,
        *late_msgs,
        scratch_shapes=[
            pltpu.VMEM((lat, width), jnp.bfloat16),
            pltpu.VMEM((lat, width), jnp.bfloat16),
            pltpu.VMEM((width, lat), jnp.float32),
            pltpu.VMEM((width, lat), jnp.float32),
        ],
    )

    terms = lax.all_to_all(terms, ORDER, 0, 0)
    grad = jax.ShapeDtypeStruct((own, wide), jnp.float32)
    key_grad, value_grad = call(settle_kernel, [grad] * 2, [VMEM], terms)

    backs = [swap(x, "g", GROUP, k) for k, x in enumerate(backs)]
    attended, query_grad = call(
        unpack_kernel,
        [low(tok, columns)] * 2,
        [VMEM] * GROUP,
        *backs,
        cost=UNPACK,
        out_spec=HBM,
        scratch_shapes=[pltpu.SemaphoreType.DMA((2 * GROUP,))],
    )
    return (attended, query_grad, key_grad, value_grad)


def solution(mesh):
    fine = Mesh(mesh.devices.reshape(tuple(SIZES.values())), AXES)
    tokens = P(AXES[:3], "tp")
    rows = P(AXES, None)
    return jax.shard_map(
        per_device,
        mesh=fine,
        in_specs=(tokens, rows, rows, P(), P(AXES[:3]), tokens),
        out_specs=(tokens, tokens, rows, rows),
        check_vma=False,
    )
```

```python
import functools
import math

import jax
import jax.numpy as jnp
from jax import lax
from jax.experimental import pallas as pl
from jax.experimental.pallas import tpu as pltpu
from jax.sharding import Mesh, PartitionSpec as P

DH = 128
TBLK = 128
BLOCKS = 2
GROUP = 8
HALVES = 1
ZSIZE = 8
TP = 4
SIZES = {"h": HALVES, "g": GROUP, "z": ZSIZE, "tp": TP}
AXES = tuple(SIZES)
ORDER = ("h", "g", "z", "tp")
MERGE = 10**11
EARLY = (4, 5, 7)
BACK_EARLY = (4, 5, 7)
UNPACK = 0
EXTRA = 16

masked_fill = -1e30
SCALE = 1.0 / DH**0.5
LOG2E = math.log2(math.e)
PARAMS = pltpu.CompilerParams(vmem_limit_bytes=32 * 2**20)
SMEM = pl.BlockSpec(memory_space=pltpu.SMEM)
VMEM = pl.BlockSpec(memory_space=pltpu.VMEM)
HBM = pl.BlockSpec(memory_space=pltpu.HBM)


def stride(axis):
    return math.prod(SIZES[a] for a in ORDER[ORDER.index(axis) + 1 :])


def source(**at):
    return sum(i * stride(axis) for axis, i in at.items())


def columns_of(k, width):
    return pl.ds(pl.multiple_of((lax.axis_index("g") ^ k) * width, width), width)


def prepare_kernel(last_ref, k_ref, v_ref, q_ref, c_ref, kv_out, *refs):
    outs, (last_s, k_s, v_s, last_sem, kv_sems, sems) = refs[:GROUP], refs[GROUP:]
    tok, width = q_ref.shape[0], outs[0].shape[1]
    small = [
        pltpu.make_async_copy(k_ref, k_s, kv_sems.at[0]),
        pltpu.make_async_copy(v_ref, v_s, kv_sems.at[1]),
        pltpu.make_async_copy(last_ref, last_s, last_sem),
    ]
    large = []
    for k, out in enumerate(outs):
        cols = columns_of(k, width)
        for i, ref in enumerate((q_ref, c_ref)):
            rows = pl.ds(i * tok, tok)
            large.append(pltpu.make_async_copy(ref.at[:, cols], out.at[rows, :], sems.at[2 * k + i]))
    for copy in small + large:
        copy.start()
    small[0].wait()
    small[1].wait()
    for t in range(TP):
        for g in range(GROUP):
            col = (t * GROUP + g) * width
            piece = jnp.concatenate([k_s[:, col : col + width], v_s[:, col : col + width]], axis=1)
            for h in range(HALVES):
                for z in range(ZSIZE):
                    kv_out[source(h=h, g=g, z=z, tp=t)] = piece
    small[2].wait()
    rows = lax.broadcasted_iota(jnp.int32, (EXTRA, width), 0)
    frames = jnp.where(rows < EXTRA // 2, last_s[0], last_s[1])
    frames = frames.astype(jnp.float32).astype(jnp.bfloat16)
    for out in outs:
        out[2 * tok : 2 * tok + EXTRA, :] = frames
    for copy in large:
        copy.wait()


def merge_kernel(*refs):
    for j, ref in enumerate(refs[:-1]):
        refs[-1][j] = ref[...]


def unpack_kernel(*refs):
    blocks, (att_ref, dq_ref, sems) = refs[:GROUP], refs[GROUP:]
    tok, width = att_ref.shape[0], blocks[0].shape[1]
    copies = []
    for k, block in enumerate(blocks):
        for i, out in enumerate((att_ref, dq_ref)):
            rows = pl.ds(i * tok, tok)
            cols = columns_of(k, width)
            copies.append(pltpu.make_async_copy(block.at[rows, :], out.at[:, cols], sems.at[2 * k + i]))
    for copy in copies:
        copy.start()
    for copy in copies:
        copy.wait()


def settle_kernel(in_ref, k_ref, v_ref):
    width = in_ref.shape[2] // 2
    for g in range(GROUP):
        for t in range(TP):
            total = jnp.zeros(in_ref.shape[1:], jnp.float32)
            for h in range(HALVES):
                for z in range(ZSIZE):
                    total += in_ref[source(h=h, g=g, z=z, tp=t)].astype(jnp.float32)
            col = (t * GROUP + g) * width
            k_ref[:, col : col + width] = total[:, 0:width]
            v_ref[:, col : col + width] = total[:, width:]


def dot(a, b, dims):
    return lax.dot_general(a, b, (dims, ((), ())), preferred_element_type=jnp.float32)


def attention_kernel(gate_ref, kv_ref, early_ref, *refs):
    late = GROUP - len(EARLY)
    late_refs, outs = refs[:late], refs[late : late + GROUP]
    grad_ref, k_s, v_s, dk_s, dv_s = refs[late + GROUP :]
    msgs = {k: early_ref.at[i] for i, k in enumerate(EARLY)}
    msgs |= zip((k for k in range(GROUP) if k not in EARLY), late_refs)
    tok = outs[0].shape[0] // 2
    lat, width = k_s.shape
    own = kv_ref.shape[1]
    gate = gate_ref[0]
    k_s[...] = kv_ref[:, :, 0:width].reshape(lat, width)
    v_s[...] = kv_ref[:, :, width:].reshape(lat, width)
    place = lax.broadcasted_iota(jnp.int32, (1, lat), 1) // own
    frame = place // stride("h") % HALVES * GROUP + place // stride("g") % GROUP
    frame = frame.astype(jnp.float32)

    def bias(j, i):
        row = 2 * tok + i * (EXTRA // 2)
        last = msgs[j][row : row + 1, 0:DH].astype(jnp.float32)
        return jnp.where(frame <= jnp.concatenate([last] * (lat // DH), axis=1), 0.0, masked_fill)

    def load(first, h):
        blocks = range(first, first + BLOCKS)
        cols = slice(h * DH, (h + 1) * DH)
        q = jnp.concatenate([msgs[j][0:tok, cols] for j in blocks], axis=0)
        cot = jnp.concatenate([msgs[j][tok : 2 * tok, cols] for j in blocks], axis=0)
        gcot = (gate * cot.astype(jnp.float32)).astype(jnp.bfloat16)
        return blocks, cols, q, gcot, k_s[:, cols], v_s[:, cols]

    def softmax(chain):
        blocks, _, q, _, keys, _ = chain
        scores = dot(q, keys, ((1,), (1,)))
        biases = [bias(j, i) for j in blocks for i in range(tok // TBLK)]
        parts = [
            scores[i * TBLK : (i + 1) * TBLK] * (SCALE * LOG2E) + b for i, b in enumerate(biases)
        ]
        scores = jnp.concatenate(parts, axis=0)
        expo = jnp.exp2(scores - jnp.max(scores, axis=-1, keepdims=True))
        return expo * (1.0 / jnp.sum(expo, axis=-1, keepdims=True))

    def prob_grads(chain):
        return dot(chain[3], chain[5], ((1,), (1,)))

    def score_grads(weights, grads):
        inner = jnp.sum(weights * grads, axis=-1, keepdims=True)
        return (weights * (grads - inner)).astype(jnp.bfloat16)

    def finish(chain, low, sgrad):
        blocks, cols, q, gcot, keys, values = chain
        out = (gate * dot(low, values, ((1,), (0,)))).astype(jnp.bfloat16)
        for i, j in enumerate(blocks):
            outs[j][0:tok, cols] = out[i * tok : (i + 1) * tok]
        out = (SCALE * dot(sgrad, keys, ((1,), (0,)))).astype(jnp.bfloat16)
        for i, j in enumerate(blocks):
            outs[j][tok : 2 * tok, cols] = out[i * tok : (i + 1) * tok]
        dk = dot(q.T, sgrad, ((1,), (0,)))
        dv = dot(gcot.T, low, ((1,), (0,)))
        dk_s[cols, :] = dk if blocks[0] == 0 else dk_s[cols, :] + dk
        dv_s[cols, :] = dv if blocks[0] == 0 else dv_s[cols, :] + dv

    chains = [(j, h) for j in range(0, GROUP, BLOCKS) for h in range(width // DH)]
    for i in range(0, len(chains), 2):
        one, two = load(*chains[i]), load(*chains[i + 1])
        weights1, grads1 = softmax(one), prob_grads(one)
        weights2 = softmax(two)
        low1, sgrad1 = weights1.astype(jnp.bfloat16), score_grads(weights1, grads1)
        grads2 = prob_grads(two)
        finish(one, low1, sgrad1)
        low2, sgrad2 = weights2.astype(jnp.bfloat16), score_grads(weights2, grads2)
        finish(two, low2, sgrad2)
    for i, grads in enumerate((SCALE * dk_s[...], dv_s[...])):
        piece = grads.T.astype(jnp.bfloat16).reshape(lat // own, own, width)
        grad_ref[:, :, i * width : (i + 1) * width] = piece


def call(kernel, shapes, specs, *args, cost=0, out_spec=VMEM, **kwargs):
    if cost:
        kwargs["cost_estimate"] = pl.CostEstimate(flops=cost, bytes_accessed=0, transcendentals=0)
    name = kernel.__name__.removesuffix("_kernel")
    out_specs = [out_spec] * len(shapes)
    return pl.pallas_call(
        kernel,
        out_shape=shapes,
        in_specs=specs,
        out_specs=out_specs,
        compiler_params=PARAMS,
        name=name,
        **kwargs,
    )(*args)


def swap(x, axis, size, k):
    return x if k == 0 else lax.ppermute(x, axis, [(i, i ^ k) for i in range(size)])


def per_device(queries, latent_keys, latent_values, gate_logit, last_frame, cotangent):
    tok, columns = queries.shape
    own, wide = latent_keys.shape
    width = columns // GROUP
    devices = HALVES * GROUP * ZSIZE * TP
    lat = own * devices
    gate = jnp.tanh(gate_logit).astype(jnp.float32).reshape(1)

    def low(*shape):
        return jax.ShapeDtypeStruct(shape, jnp.bfloat16)

    kv_shape = low(devices, own, 2 * width)
    last_frame, latent_keys, latent_values, queries, cotangent = (
        pltpu.with_memory_space_constraint(x, pltpu.HBM)
        for x in (last_frame, latent_keys, latent_values, queries, cotangent)
    )
    both, *msgs = call(
        prepare_kernel,
        [kv_shape] + [low(2 * tok + EXTRA, width)] * GROUP,
        [HBM] * 5,
        last_frame,
        latent_keys,
        latent_values,
        queries,
        cotangent,
        scratch_shapes=[
            pltpu.SMEM((last_frame.shape[0],), jnp.int32),
            pltpu.VMEM((own, wide), jnp.bfloat16),
            pltpu.VMEM((own, wide), jnp.bfloat16),
            pltpu.SemaphoreType.DMA,
            pltpu.SemaphoreType.DMA((2,)),
            pltpu.SemaphoreType.DMA((2 * GROUP,)),
        ],
    )
    both = lax.all_to_all(both, ORDER, 0, 0)
    msgs = [swap(x, "g", GROUP, k) for k, x in enumerate(msgs)]
    early = low(len(EARLY), 2 * tok + EXTRA, width)
    early_msgs = [msgs[k] for k in EARLY]
    (early,) = call(merge_kernel, [early], [VMEM] * len(EARLY), *early_msgs, cost=MERGE)
    late_msgs = [x for k, x in enumerate(msgs) if k not in EARLY]

    *backs, terms = call(
        attention_kernel,
        [low(2 * tok, width)] * GROUP + [kv_shape],
        [SMEM] + [VMEM] * (2 + len(late_msgs)),
        gate,
        both,
        early,
        *late_msgs,
        scratch_shapes=[
            pltpu.VMEM((lat, width), jnp.bfloat16),
            pltpu.VMEM((lat, width), jnp.bfloat16),
            pltpu.VMEM((width, lat), jnp.float32),
            pltpu.VMEM((width, lat), jnp.float32),
        ],
    )

    terms = lax.all_to_all(terms, ORDER, 0, 0)
    grad = jax.ShapeDtypeStruct((own, wide), jnp.float32)
    key_grad, value_grad = call(settle_kernel, [grad] * 2, [VMEM], terms)

    backs = [swap(x, "g", GROUP, k) for k, x in enumerate(backs)]
    if BACK_EARLY:
        shape = low(len(BACK_EARLY), 2 * tok, width)
        some = [backs[k] for k in BACK_EARLY]
        (some,) = call(merge_kernel, [shape], [VMEM] * len(some), *some, cost=MERGE)
        for i, k in enumerate(BACK_EARLY):
            backs[k] = some[i]
    attended, query_grad = call(
        unpack_kernel,
        [low(tok, columns)] * 2,
        [VMEM] * GROUP,
        *backs,
        cost=UNPACK,
        out_spec=HBM,
        scratch_shapes=[pltpu.SemaphoreType.DMA((2 * GROUP,))],
    )
    return (attended, query_grad, key_grad, value_grad)


def solution(mesh):
    fine = Mesh(mesh.devices.reshape(tuple(SIZES.values())), AXES)
    tokens = P(AXES[:3], "tp")
    rows = P(AXES, None)
    return jax.shard_map(
        per_device,
        mesh=fine,
        in_specs=(tokens, rows, rows, P(), P(AXES[:3]), tokens),
        out_specs=(tokens, tokens, rows, rows),
        check_vma=False,
    )
```

```python
import functools
import math

import jax
import jax.numpy as jnp
from jax import lax
from jax.experimental import pallas as pl
from jax.experimental.pallas import tpu as pltpu
from jax.sharding import Mesh, PartitionSpec as P

DH = 128
TBLK = 128
BLOCKS = 4
GROUP = 8
HALVES = 1
ZSIZE = 8
TP = 4
SIZES = {"h": HALVES, "g": GROUP, "z": ZSIZE, "tp": TP}
AXES = tuple(SIZES)
ORDER = ("h", "g", "z", "tp")
MERGE = 10**11
EARLY = (4, 5, 7)
BACK_EARLY = (4, 5, 7)
UNPACK = 0
EXTRA = 16

masked_fill = -1e30
SCALE = 1.0 / DH**0.5
LOG2E = math.log2(math.e)
PARAMS = pltpu.CompilerParams(vmem_limit_bytes=32 * 2**20)
SMEM = pl.BlockSpec(memory_space=pltpu.SMEM)
VMEM = pl.BlockSpec(memory_space=pltpu.VMEM)
HBM = pl.BlockSpec(memory_space=pltpu.HBM)


def stride(axis):
    return math.prod(SIZES[a] for a in ORDER[ORDER.index(axis) + 1 :])


def source(**at):
    return sum(i * stride(axis) for axis, i in at.items())


def columns_of(k, width):
    return pl.ds(pl.multiple_of((lax.axis_index("g") ^ k) * width, width), width)


def prepare_kernel(last_ref, k_ref, v_ref, q_ref, c_ref, kv_out, *refs):
    outs, (last_s, k_s, v_s, last_sem, kv_sems, sems) = refs[:GROUP], refs[GROUP:]
    tok, width = q_ref.shape[0], outs[0].shape[1]
    small = [
        pltpu.make_async_copy(k_ref, k_s, kv_sems.at[0]),
        pltpu.make_async_copy(v_ref, v_s, kv_sems.at[1]),
        pltpu.make_async_copy(last_ref, last_s, last_sem),
    ]
    large = []
    for k, out in enumerate(outs):
        cols = columns_of(k, width)
        for i, ref in enumerate((q_ref, c_ref)):
            rows = pl.ds(i * tok, tok)
            large.append(pltpu.make_async_copy(ref.at[:, cols], out.at[rows, :], sems.at[2 * k + i]))
    for copy in small + large:
        copy.start()
    small[0].wait()
    small[1].wait()
    for t in range(TP):
        for g in range(GROUP):
            col = (t * GROUP + g) * width
            piece = jnp.concatenate([k_s[:, col : col + width], v_s[:, col : col + width]], axis=1)
            for h in range(HALVES):
                for z in range(ZSIZE):
                    kv_out[source(h=h, g=g, z=z, tp=t)] = piece
    small[2].wait()
    rows = lax.broadcasted_iota(jnp.int32, (EXTRA, width), 0)
    frames = jnp.where(rows < EXTRA // 2, last_s[0], last_s[1])
    frames = frames.astype(jnp.float32).astype(jnp.bfloat16)
    for out in outs:
        out[2 * tok : 2 * tok + EXTRA, :] = frames
    for copy in large:
        copy.wait()


def merge_kernel(*refs):
    for j, ref in enumerate(refs[:-1]):
        refs[-1][j] = ref[...]


def unpack_kernel(*refs):
    blocks, (att_ref, dq_ref, sems) = refs[:GROUP], refs[GROUP:]
    tok, width = att_ref.shape[0], blocks[0].shape[1]
    copies = []
    for k, block in enumerate(blocks):
        for i, out in enumerate((att_ref, dq_ref)):
            rows = pl.ds(i * tok, tok)
            cols = columns_of(k, width)
            copies.append(pltpu.make_async_copy(block.at[rows, :], out.at[:, cols], sems.at[2 * k + i]))
    for copy in copies:
        copy.start()
    for copy in copies:
        copy.wait()


def settle_kernel(in_ref, k_ref, v_ref):
    width = in_ref.shape[2] // 2
    for g in range(GROUP):
        for t in range(TP):
            total = jnp.zeros(in_ref.shape[1:], jnp.float32)
            for h in range(HALVES):
                for z in range(ZSIZE):
                    total += in_ref[source(h=h, g=g, z=z, tp=t)].astype(jnp.float32)
            col = (t * GROUP + g) * width
            k_ref[:, col : col + width] = total[:, 0:width]
            v_ref[:, col : col + width] = total[:, width:]


def dot(a, b, dims):
    return lax.dot_general(a, b, (dims, ((), ())), preferred_element_type=jnp.float32)


def attention_kernel(gate_ref, kv_ref, early_ref, *refs):
    late = GROUP - len(EARLY)
    late_refs, outs = refs[:late], refs[late : late + GROUP]
    grad_ref, k_s, v_s, dk_s, dv_s = refs[late + GROUP :]
    msgs = {k: early_ref.at[i] for i, k in enumerate(EARLY)}
    msgs |= zip((k for k in range(GROUP) if k not in EARLY), late_refs)
    tok = outs[0].shape[0] // 2
    lat, width = k_s.shape
    own = kv_ref.shape[1]
    gate = gate_ref[0]
    k_s[...] = kv_ref[:, :, 0:width].reshape(lat, width)
    v_s[...] = kv_ref[:, :, width:].reshape(lat, width)
    place = lax.broadcasted_iota(jnp.int32, (1, lat), 1) // own
    frame = place // stride("h") % HALVES * GROUP + place // stride("g") % GROUP
    frame = frame.astype(jnp.float32)

    def bias(j, i):
        row = 2 * tok + i * (EXTRA // 2)
        last = msgs[j][row : row + 1, 0:DH].astype(jnp.float32)
        return jnp.where(frame <= jnp.concatenate([last] * (lat // DH), axis=1), 0.0, masked_fill)

    def load(first, h):
        blocks = range(first, first + BLOCKS)
        cols = slice(h * DH, (h + 1) * DH)
        q = jnp.concatenate([msgs[j][0:tok, cols] for j in blocks], axis=0)
        cot = jnp.concatenate([msgs[j][tok : 2 * tok, cols] for j in blocks], axis=0)
        gcot = (gate * cot.astype(jnp.float32)).astype(jnp.bfloat16)
        return blocks, cols, q, gcot, k_s[:, cols], v_s[:, cols]

    def softmax(chain):
        blocks, _, q, _, keys, _ = chain
        scores = dot(q, keys, ((1,), (1,)))
        biases = [bias(j, i) for j in blocks for i in range(tok // TBLK)]
        parts = [
            scores[i * TBLK : (i + 1) * TBLK] * (SCALE * LOG2E) + b for i, b in enumerate(biases)
        ]
        scores = jnp.concatenate(parts, axis=0)
        expo = jnp.exp2(scores - jnp.max(scores, axis=-1, keepdims=True))
        return expo * (1.0 / jnp.sum(expo, axis=-1, keepdims=True))

    def prob_grads(chain):
        return dot(chain[3], chain[5], ((1,), (1,)))

    def score_grads(weights, grads):
        inner = jnp.sum(weights * grads, axis=-1, keepdims=True)
        return (weights * (grads - inner)).astype(jnp.bfloat16)

    def finish(chain, low, sgrad):
        blocks, cols, q, gcot, keys, values = chain
        out = (gate * dot(low, values, ((1,), (0,)))).astype(jnp.bfloat16)
        for i, j in enumerate(blocks):
            outs[j][0:tok, cols] = out[i * tok : (i + 1) * tok]
        out = (SCALE * dot(sgrad, keys, ((1,), (0,)))).astype(jnp.bfloat16)
        for i, j in enumerate(blocks):
            outs[j][tok : 2 * tok, cols] = out[i * tok : (i + 1) * tok]
        dk = dot(q.T, sgrad, ((1,), (0,)))
        dv = dot(gcot.T, low, ((1,), (0,)))
        dk_s[cols, :] = dk if blocks[0] == 0 else dk_s[cols, :] + dk
        dv_s[cols, :] = dv if blocks[0] == 0 else dv_s[cols, :] + dv

    chains = [(j, h) for j in range(0, GROUP, BLOCKS) for h in range(width // DH)]
    for i in range(0, len(chains), 2):
        one, two = load(*chains[i]), load(*chains[i + 1])
        weights1, grads1 = softmax(one), prob_grads(one)
        weights2 = softmax(two)
        low1, sgrad1 = weights1.astype(jnp.bfloat16), score_grads(weights1, grads1)
        grads2 = prob_grads(two)
        finish(one, low1, sgrad1)
        low2, sgrad2 = weights2.astype(jnp.bfloat16), score_grads(weights2, grads2)
        finish(two, low2, sgrad2)
    for i, grads in enumerate((SCALE * dk_s[...], dv_s[...])):
        piece = grads.T.astype(jnp.bfloat16).reshape(lat // own, own, width)
        grad_ref[:, :, i * width : (i + 1) * width] = piece


def call(kernel, shapes, specs, *args, cost=0, out_spec=VMEM, **kwargs):
    if cost:
        kwargs["cost_estimate"] = pl.CostEstimate(flops=cost, bytes_accessed=0, transcendentals=0)
    name = kernel.__name__.removesuffix("_kernel")
    out_specs = [out_spec] * len(shapes)
    return pl.pallas_call(
        kernel,
        out_shape=shapes,
        in_specs=specs,
        out_specs=out_specs,
        compiler_params=PARAMS,
        name=name,
        **kwargs,
    )(*args)


def swap(x, axis, size, k):
    return x if k == 0 else lax.ppermute(x, axis, [(i, i ^ k) for i in range(size)])


def per_device(queries, latent_keys, latent_values, gate_logit, last_frame, cotangent):
    tok, columns = queries.shape
    own, wide = latent_keys.shape
    width = columns // GROUP
    devices = HALVES * GROUP * ZSIZE * TP
    lat = own * devices
    gate = jnp.tanh(gate_logit).astype(jnp.float32).reshape(1)

    def low(*shape):
        return jax.ShapeDtypeStruct(shape, jnp.bfloat16)

    kv_shape = low(devices, own, 2 * width)
    last_frame, latent_keys, latent_values, queries, cotangent = (
        pltpu.with_memory_space_constraint(x, pltpu.HBM)
        for x in (last_frame, latent_keys, latent_values, queries, cotangent)
    )
    both, *msgs = call(
        prepare_kernel,
        [kv_shape] + [low(2 * tok + EXTRA, width)] * GROUP,
        [HBM] * 5,
        last_frame,
        latent_keys,
        latent_values,
        queries,
        cotangent,
        scratch_shapes=[
            pltpu.SMEM((last_frame.shape[0],), jnp.int32),
            pltpu.VMEM((own, wide), jnp.bfloat16),
            pltpu.VMEM((own, wide), jnp.bfloat16),
            pltpu.SemaphoreType.DMA,
            pltpu.SemaphoreType.DMA((2,)),
            pltpu.SemaphoreType.DMA((2 * GROUP,)),
        ],
    )
    both = lax.all_to_all(both, ORDER, 0, 0)
    msgs = [swap(x, "g", GROUP, k) for k, x in enumerate(msgs)]
    early = low(len(EARLY), 2 * tok + EXTRA, width)
    early_msgs = [msgs[k] for k in EARLY]
    (early,) = call(merge_kernel, [early], [VMEM] * len(EARLY), *early_msgs, cost=MERGE)
    late_msgs = [x for k, x in enumerate(msgs) if k not in EARLY]

    *backs, terms = call(
        attention_kernel,
        [low(2 * tok, width)] * GROUP + [kv_shape],
        [SMEM] + [VMEM] * (2 + len(late_msgs)),
        gate,
        both,
        early,
        *late_msgs,
        scratch_shapes=[
            pltpu.VMEM((lat, width), jnp.bfloat16),
            pltpu.VMEM((lat, width), jnp.bfloat16),
            pltpu.VMEM((width, lat), jnp.float32),
            pltpu.VMEM((width, lat), jnp.float32),
        ],
    )

    terms = lax.all_to_all(terms, ORDER, 0, 0)
    grad = jax.ShapeDtypeStruct((own, wide), jnp.float32)
    key_grad, value_grad = call(settle_kernel, [grad] * 2, [VMEM], terms)

    backs = [swap(x, "g", GROUP, k) for k, x in enumerate(backs)]
    if BACK_EARLY:
        shape = low(len(BACK_EARLY), 2 * tok, width)
        some = [backs[k] for k in BACK_EARLY]
        (some,) = call(merge_kernel, [shape], [VMEM] * len(some), *some, cost=MERGE)
        for i, k in enumerate(BACK_EARLY):
            backs[k] = some[i]
    attended, query_grad = call(
        unpack_kernel,
        [low(tok, columns)] * 2,
        [VMEM] * GROUP,
        *backs,
        cost=UNPACK,
        out_spec=HBM,
        scratch_shapes=[pltpu.SemaphoreType.DMA((2 * GROUP,))],
    )
    return (attended, query_grad, key_grad, value_grad)


def solution(mesh):
    fine = Mesh(mesh.devices.reshape(tuple(SIZES.values())), AXES)
    tokens = P(AXES[:3], "tp")
    rows = P(AXES, None)
    return jax.shard_map(
        per_device,
        mesh=fine,
        in_specs=(tokens, rows, rows, P(), P(AXES[:3]), tokens),
        out_specs=(tokens, tokens, rows, rows),
        check_vma=False,
    )
```
